256 devices in a mesh: pipe: 4 (over y), tensor: 32 (over z, x), dp: 2 (over core).
Axes of the slice: x: 4, y: 4, z: 8, core: 2. Of those that a mesh axis runs over, the one named last changes fastest.
Arguments:
- states: bfloat16 [4, 2, 128, 4096], P('pipe', 'dp', 'tensor'), may hold values from -6 to 6
- out_grad: bfloat16 [2, 128, 4096], P('dp', 'tensor'), may hold values from -6 to 6
- norm_gain: bfloat16 [4, 4096], P('pipe'), may hold values from 0.5 to 1.5
- gate_tiles: bfloat16 [4, 3520, 128, 128], P('pipe', 'tensor'), may hold values from -0.125 to 0.125
- up_tiles: bfloat16 [4, 3520, 128, 128], P('pipe', 'tensor'), may hold values from -0.125 to 0.125
- down_tiles: bfloat16 [4, 3520, 128, 128], P('pipe', 'tensor'), may hold values from -0.0625 to 0.0625
- tile_lists: int32 [4, 3, 3520, 2], P('pipe', None, 'tensor'), may hold values from 0 to 31, as said below
- tile_counts: int32 [4, 3, 32], P('pipe', None, 'tensor'), may hold values from 50 to 110, as said below
- gate_a: bfloat16 [4, 4096, 64], P('pipe'), may hold values from -0.09375 to 0.09375
- gate_adapter_output: bfloat16 [4, 64, 20480], P('pipe', None, 'tensor'), may hold values from -0.75 to 0.75
- up_a: bfloat16 [4, 4096, 64], P('pipe'), may hold values from -0.09375 to 0.09375
- upper_adapter_output: bfloat16 [4, 64, 20480], P('pipe', None, 'tensor'), may hold values from -0.75 to 0.75
- down_adapter_input: bfloat16 [4, 20480, 64], P('pipe', 'tensor'), may hold values from -0.0390625 to 0.0390625
- down_b: bfloat16 [4, 64, 4096], P('pipe'), may hold values from -0.75 to 0.75
Outputs:
- section_grads: bfloat16 [4, 2, 128, 4096], P('pipe', 'dp', 'tensor')
- grad_gate_a: bfloat16 [4, 4096, 64], P('pipe')
- grad_gate_b: bfloat16 [4, 64, 20480], P('pipe', None, 'tensor')
- grad_up_a: bfloat16 [4, 4096, 64], P('pipe')
- grad_up_b: bfloat16 [4, 64, 20480], P('pipe', None, 'tensor')
- grad_down_a: bfloat16 [4, 20480, 64], P('pipe', 'tensor')
- grad_down_b: bfloat16 [4, 64, 4096], P('pipe')
The draws below stay inside these ranges and needn't reach their ends.
Inputs may be any that keep to these rules, and one draw needn't show every extreme that they name: `tile_counts`: entry [s, p, j] counts the kept tiles of shard j of projection p at section s; shard j and the shard half the tensor axis away keep exactly 160 tiles together. `tile_lists`: entries [s, p, j * 110 + k] give (row block, column block) of stored tile k of shard j, within the shard's own blocks; for gate and up the rows run over the 4096 features, for down over the shard's hidden units. The first counted entries of a shard name distinct blocks; the rest are unused.
All inputs are finite; a program needn't handle non-finite values.
Results may differ from the reference program's by a relative error of at most 0.035.
Values may be sent and summed in bfloat16 or wider, within the bound.
A program may use at most 192 MiB of HBM per device.

```python
import jax
import jax.numpy as jnp
from jax import lax

D = 4096
FF = 20480
R = 64
TILE = 128
TOKENS_MB = 128
MICRO = 2
KEEP = 80
SPREAD = 30
KMAX = 110
N_PIPE = 4
N_TENSOR = 32


def tile_plan(key):
    row_blocks = D // TILE
    col_blocks = FF // N_TENSOR // TILE
    total_tiles = row_blocks * col_blocks
    half_axis = N_TENSOR // 2
    key_shift, key_pick, key_sign, key_order = jax.random.split(key, 4)
    shifts = jax.random.randint(key_shift, (N_PIPE, 3, half_axis), -SPREAD, SPREAD + 1)
    picked = jax.random.randint(key_pick, (N_PIPE, 3, 1), 0, half_axis)
    signs = 2 * jax.random.randint(key_sign, (N_PIPE, 3, 1), 0, 2) - 1
    shifts = jnp.where(jnp.arange(half_axis)[None, None, :] == picked, SPREAD * signs, shifts)
    counts = jnp.concatenate([KEEP + shifts, KEEP - shifts], axis=2).astype(jnp.int32)
    base = jnp.broadcast_to(jnp.arange(total_tiles, dtype=jnp.int32), (N_PIPE, 3, N_TENSOR, total_tiles))
    ordered = jax.random.permutation(key_order, base, axis=3, independent=True)[..., :KMAX]
    widths = jnp.array([col_blocks, col_blocks, row_blocks], dtype=jnp.int32)[None, :, None, None]
    lists = jnp.stack([ordered // widths, ordered % widths], axis=-1).reshape(N_PIPE, 3, N_TENSOR * KMAX, 2)
    return (counts, lists.astype(jnp.int32))


def draw_tile_counts(key, part):
    return tile_plan(key)[0]


def draw_tile_lists(key, part):
    return tile_plan(key)[1]


def level_of(rng, dims, cuts, smallest, high):
    level = 1.0
    for dim, parts in cuts:
        steps = jax.random.uniform(jax.random.fold_in(jax.random.fold_in(rng, 6), dim), (parts,), jnp.float32, smallest / len(cuts), high / len(cuts))
        level = level * jnp.repeat(jnp.exp(steps), dims[dim] // parts).reshape((-1,) + (1,) * (len(dims) - 1 - dim))
    return level


def normal_values(key, dims, spread, most, cuts=(), held_as=jnp.bfloat16):
    loudness = level_of(key, dims, cuts, -0.22, 0.18) if cuts else 1.0
    entries = jax.random.normal(key, dims, jnp.float32) * spread * loudness
    return jnp.minimum(jnp.maximum(entries, -most), most).astype(held_as)


def setup_inputs(seed: int = 0) -> dict:
    arg_keys = jax.random.split(jax.random.key(seed), 15)
    states = normal_values(arg_keys[0], (N_PIPE, MICRO, TOKENS_MB, D), 1.0, 6.0, ((0, 4), (1, 2), (2, 32)))
    out_grad = normal_values(arg_keys[1], (MICRO, TOKENS_MB, D), 1.0, 6.0, ((0, 2), (1, 32)))
    norm_gain = jnp.clip(1.0 + 0.1 * jax.random.normal(arg_keys[2], (N_PIPE, D), jnp.float32), 0.5, 1.5).astype(jnp.bfloat16)
    gate_tiles = normal_values(arg_keys[3], (N_PIPE, N_TENSOR * KMAX, TILE, TILE), (D // 2) ** -0.5, 0.125, ((0, 4), (1, 32)))
    up_tiles = normal_values(arg_keys[4], (N_PIPE, N_TENSOR * KMAX, TILE, TILE), (D // 2) ** -0.5, 0.125, ((0, 4), (1, 32)))
    down_tiles = normal_values(arg_keys[5], (N_PIPE, N_TENSOR * KMAX, TILE, TILE), (FF // 2) ** -0.5, 0.0625, ((0, 4), (1, 32)))
    tile_lists = draw_tile_lists(jax.random.fold_in(arg_keys[14], 71), 0)
    tile_counts = draw_tile_counts(jax.random.fold_in(arg_keys[14], 71), 0)
    gate_a = normal_values(arg_keys[8], (N_PIPE, D, R), D ** -0.5, 0.09375, ((0, 4),))
    gate_adapter_output = normal_values(arg_keys[9], (N_PIPE, R, FF), R ** -0.5, 0.75, ((0, 4), (2, 32)))
    up_a = normal_values(arg_keys[10], (N_PIPE, D, R), D ** -0.5, 0.09375, ((0, 4),))
    upper_adapter_output = normal_values(arg_keys[11], (N_PIPE, R, FF), R ** -0.5, 0.75, ((0, 4), (2, 32)))
    down_adapter_input = normal_values(arg_keys[12], (N_PIPE, FF, R), FF ** -0.5, 0.0390625, ((0, 4), (1, 32)))
    down_b = normal_values(arg_keys[13], (N_PIPE, R, D), R ** -0.5, 0.75, ((0, 4),))
    return dict(states=states, out_grad=out_grad, norm_gain=norm_gain, gate_tiles=gate_tiles, up_tiles=up_tiles, down_tiles=down_tiles, tile_lists=tile_lists, tile_counts=tile_counts, gate_a=gate_a, gate_adapter_output=gate_adapter_output, up_a=up_a, upper_adapter_output=upper_adapter_output, down_adapter_input=down_adapter_input, down_b=down_b)


EPSILON = 1e-05
ADAPTER_SCALE = 0.25
EXACT_PRECISION = lax.Precision.HIGHEST

def exact_product(left, right):
    return jnp.dot(left.astype(jnp.float32), right.astype(jnp.float32), precision=EXACT_PRECISION)

def silu_parts(gate_activation):
    sigmoid = jax.nn.sigmoid(gate_activation)
    return (gate_activation * sigmoid, sigmoid * (1.0 + gate_activation * (1.0 - sigmoid)))

def assemble(stacked, placed, kept, row_blocks, col_blocks):
    shards = kept.shape[0]
    slot_count = stacked.shape[0] // shards

    def one_shard(operands):
        tiles_in, places_in, kept_in = operands
        alive = (jnp.arange(slot_count).astype(jnp.int32) < kept_in).astype(jnp.float32)
        weighted = tiles_in.astype(jnp.float32) * alive[:, None, None]
        dense = jnp.zeros((row_blocks, col_blocks, TILE, TILE), jnp.float32)
        dense = dense.at[places_in[:, 0].astype(jnp.int32), places_in[:, 1].astype(jnp.int32)].add(weighted)
        return dense.transpose(0, 2, 1, 3).reshape(row_blocks * TILE, col_blocks * TILE).astype(jnp.bfloat16)
    return lax.map(one_shard, (stacked.reshape(shards, slot_count, TILE, TILE), placed.reshape(shards, slot_count, 2), kept))

def reference(states, out_grad, norm_gain, gate_tiles, up_tiles, down_tiles, tile_lists, tile_counts, gate_a, gate_adapter_output, up_a, upper_adapter_output, down_adapter_input, down_b):
    row_blocks = D // TILE
    col_blocks = FF // N_TENSOR // TILE
    current_gradient = out_grad.reshape(MICRO * TOKENS_MB, D)
    section_out = []
    output_gradients = []
    for feedforward_index in range(N_PIPE - 1, -1, -1):
        gate_weight_dense = assemble(gate_tiles[feedforward_index], tile_lists[feedforward_index, 0], tile_counts[feedforward_index, 0], row_blocks, col_blocks).transpose(1, 0, 2).reshape(D, FF)
        upper_weight_dense = assemble(up_tiles[feedforward_index], tile_lists[feedforward_index, 1], tile_counts[feedforward_index, 1], row_blocks, col_blocks).transpose(1, 0, 2).reshape(D, FF)
        down_weight_dense = assemble(down_tiles[feedforward_index], tile_lists[feedforward_index, 2], tile_counts[feedforward_index, 2], col_blocks, row_blocks).reshape(FF, D)
        inputs = states[feedforward_index].reshape(MICRO * TOKENS_MB, D).astype(jnp.float32)
        scale_rms = lax.rsqrt(lax.optimization_barrier(jnp.mean(inputs * inputs, axis=1, keepdims=True)) + EPSILON)
        normed = inputs * scale_rms
        gain_row = norm_gain[feedforward_index].astype(jnp.float32)
        normalized_narrow = (normed * gain_row).astype(jnp.bfloat16)
        gate_lowrank = exact_product(normalized_narrow, gate_a[feedforward_index]).astype(jnp.bfloat16)
        upper_lowrank = exact_product(normalized_narrow, up_a[feedforward_index]).astype(jnp.bfloat16)
        gradient_lowrank = exact_product(current_gradient, down_b[feedforward_index].T).astype(jnp.bfloat16)
        gate_activation = exact_product(normalized_narrow, gate_weight_dense) + ADAPTER_SCALE * exact_product(gate_lowrank, gate_adapter_output[feedforward_index])
        upward_projection = exact_product(normalized_narrow, upper_weight_dense) + ADAPTER_SCALE * exact_product(upper_lowrank, upper_adapter_output[feedforward_index])
        hidden_gradient = exact_product(current_gradient, down_weight_dense.T) + ADAPTER_SCALE * exact_product(gradient_lowrank, down_adapter_input[feedforward_index].T)
        active_part, slope_part = silu_parts(gate_activation)
        hidden_state = (active_part * upward_projection).astype(jnp.bfloat16)
        gate_gradient = (hidden_gradient * upward_projection * slope_part).astype(jnp.bfloat16)
        upper_gradient = (hidden_gradient * active_part).astype(jnp.bfloat16)
        gate_backward = exact_product(gate_gradient, gate_adapter_output[feedforward_index].T)
        upper_backward = exact_product(upper_gradient, upper_adapter_output[feedforward_index].T)
        reduced_total = exact_product(hidden_state, down_adapter_input[feedforward_index])
        shared_values = exact_product(gate_gradient, gate_weight_dense.T) + exact_product(upper_gradient, upper_weight_dense.T)
        shared_values = shared_values + ADAPTER_SCALE * (exact_product(gate_backward, gate_a[feedforward_index].T) + exact_product(upper_backward, up_a[feedforward_index].T))
        scaled = shared_values * gain_row
        branch = scale_rms * (scaled - normed * lax.optimization_barrier(jnp.mean(scaled * normed, axis=1, keepdims=True)))
        result = (current_gradient.astype(jnp.float32) + branch).astype(jnp.bfloat16)
        output_gradients.append(((ADAPTER_SCALE * exact_product(normalized_narrow.T, gate_backward)).astype(jnp.bfloat16), (ADAPTER_SCALE * exact_product(gate_lowrank.T, gate_gradient)).astype(jnp.bfloat16), (ADAPTER_SCALE * exact_product(normalized_narrow.T, upper_backward)).astype(jnp.bfloat16), (ADAPTER_SCALE * exact_product(upper_lowrank.T, upper_gradient)).astype(jnp.bfloat16), (ADAPTER_SCALE * exact_product(hidden_state.T, gradient_lowrank)).astype(jnp.bfloat16), (ADAPTER_SCALE * exact_product(reduced_total.T, current_gradient)).astype(jnp.bfloat16)))
        section_out.append(result.reshape(MICRO, TOKENS_MB, D))
        current_gradient = result
    section_out = section_out[::-1]
    output_gradients = output_gradients[::-1]
    stacked_grads = [jnp.stack([entry[member] for entry in output_gradients]) for member in range(6)]
    return (jnp.stack(section_out), stacked_grads[0], stacked_grads[1], stacked_grads[2], stacked_grads[3], stacked_grads[4], stacked_grads[5])
```

```python
import functools

import jax
import jax.numpy as jnp
from jax import lax
from jax.experimental import pallas as pl
from jax.experimental.pallas import tpu as pltpu
from jax.sharding import PartitionSpec as P

MESH = pl.DeviceIdType.MESH
F32 = jnp.float32
BF16 = jnp.bfloat16
EPSILON = 1e-05
SCALE = 0.25
X_CHIPS = 4
TILE = 128
EXTRA = 256


def dot_nn(a, b):
    return lax.dot_general(a, b, (((1,), (0,)), ((), ())), preferred_element_type=F32)


def dot_nt(a, b):
    return lax.dot_general(a, b, (((1,), (1,)), ((), ())), preferred_element_type=F32)


def dot_tn(a, b):
    return lax.dot_general(a, b, (((0,), (0,)), ((), ())), preferred_element_type=F32)


def each(count, body):
    def step(i, carry):
        body(i)
        return carry

    lax.fori_loop(0, count, step, 0)


def aligned(index, size):
    return pl.ds(pl.multiple_of(index * size, size), size)


def section_kernel(
    sizes,
    inv,
    x_ref,
    go_ref,
    gain_ref,
    gate_hbm,
    up_hbm,
    down_hbm,
    ab_hbm,
    gb_ref,
    ub_ref,
    da_ref,
    db_hbm,
    dx_out,
    ab_out,
    hid_out,
    da_out,
    db_out,
    tiles_g,
    tiles_u,
    tiles_d,
    wg,
    wu,
    wd,
    gbx,
    ubx,
    dax,
    a2a_send,
    a2a_recv,
    n16,
    r16,
    u_all,
    g_all,
    acc_g,
    acc_u,
    acc_d,
    a_gu,
    c_lr,
    hid,
    dge,
    dup,
    tm,
    slab_send,
    slab_recv,
    total,
    z_send,
    z_recv,
    dx16,
    dx32,
    o_send,
    o_recv,
    t_all,
    pa_send,
    pa_recv,
    pb_send,
    pb_recv,
    ps_send,
    ps_recv,
    pd_send,
    pd_recv,
    load_sem,
    a2a_ss,
    a2a_rs,
    uz_ss,
    uz_rs,
    ux_ss,
    ux_rs,
    gz_ss,
    gz_rs,
    gx_ss,
    gx_rs,
    y_ss,
    y_rs,
    rx_ss,
    rx_rs,
    rz_ss,
    rz_rs,
    o_ss,
    o_rs,
    tz_ss,
    tz_rs,
    dp_ss,
    dp_rs,
):
    pipe_n, nz, nx, hidden, width = sizes
    slab = width // nx
    rows_q = x_ref.shape[0]
    zt = rows_q * nx
    col_blocks = hidden // TILE
    row_blocks = width // TILE
    rank = gb_ref.shape[0]
    pipe = lax.axis_index("pipe")
    tensor = lax.axis_index("tensor")
    core = lax.axis_index("dp")
    z = tensor // nx
    x = lax.rem(tensor, nx)

    def remote(src, dst, ss, rs, **where):
        return pltpu.make_async_remote_copy(
            src_ref=src, dst_ref=dst, send_sem=ss, recv_sem=rs, device_id=where, device_id_type=MESH
        )

    def x_peer(i):
        return z * nx + lax.rem(x + i, nx)

    def z_peer(i):
        return lax.rem(z + i, nz) * nx + x

    barrier = pltpu.get_barrier_semaphore()

    def greet(**where):
        pl.semaphore_signal(barrier, inc=1, device_id=where, device_id_type=MESH)

    each(nx - 1, lambda i: greet(tensor=x_peer(i + 1)))
    each(nz - 1, lambda i: greet(tensor=z_peer(i + 1)))
    greet(dp=1 - core)
    greet(pipe=lax.rem(pipe + 1, pipe_n))
    greet(pipe=lax.rem(pipe + pipe_n - 1, pipe_n))

    loads = [
        pltpu.make_async_copy(gate_hbm, tiles_g, load_sem.at[0]),
        pltpu.make_async_copy(up_hbm, tiles_u, load_sem.at[1]),
        pltpu.make_async_copy(down_hbm, tiles_d, load_sem.at[2]),
        pltpu.make_async_copy(ab_hbm, wg.at[:, pl.ds(hidden, TILE)], load_sem.at[3]),
        pltpu.make_async_copy(db_hbm, wd.at[pl.ds(hidden, rank), :], load_sem.at[4]),
    ]
    for load in loads:
        load.start()

    xin = x_ref[...].astype(F32)
    scale_rms = lax.rsqrt(jnp.mean(xin * xin, axis=1, keepdims=True) + EPSILON)
    normed = xin * scale_rms
    given = go_ref[...].astype(F32)
    for k in range(nx):
        a2a_send[k, :, 0:slab] = normed[:, k * slab : (k + 1) * slab]
        a2a_send[k, :, slab : 2 * slab] = given[:, k * slab : (k + 1) * slab]
        a2a_send[k, :, 2 * slab : 2 * slab + TILE] = jnp.broadcast_to(scale_rms, (rows_q, TILE))

    pl.semaphore_wait(barrier, (nx - 1) + (nz - 1) + 3)

    def a2a(i):
        return remote(
            a2a_send.at[lax.rem(x + i + 1, nx)],
            a2a_recv.at[x],
            a2a_ss.at[i],
            a2a_rs.at[i],
            tensor=x_peer(i + 1),
        )

    each(nx - 1, lambda i: a2a(i).start())
    a2a_recv[x] = a2a_send[x]
    each(nx - 1, lambda i: a2a(i).wait())
    for k in range(nx):
        n16[k * rows_q : (k + 1) * rows_q, :] = a2a_recv[k, :, 0:slab]
        dx32[k * rows_q : (k + 1) * rows_q, :] = a2a_recv[k, :, slab : 2 * slab]
        r16[k * rows_q : (k + 1) * rows_q, :] = a2a_recv[k, :, 2 * slab : 2 * slab + TILE]
    gain = gain_ref[:, aligned(x, slab)].astype(F32)
    mine = aligned(z, zt)
    u_all[x, mine, :] = (n16[...] * gain).astype(BF16)

    def gather_z(buf, ss, rs, i):
        return remote(
            buf.at[x, mine], buf.at[x, mine], ss.at[i], rs.at[i], tensor=z_peer(i + 1)
        )

    def gather_x(buf, ss, rs, i):
        return remote(buf.at[x], buf.at[x], ss.at[i], rs.at[i], tensor=x_peer(i + 1))

    def u_z(i):
        return gather_z(u_all, uz_ss, uz_rs, i)

    def u_x(i):
        return gather_x(u_all, ux_ss, ux_rs, i)

    def g_z(i):
        return gather_z(g_all, gz_ss, gz_rs, i)

    def g_x(i):
        return gather_x(g_all, gx_ss, gx_rs, i)

    last = pipe == pipe_n - 1

    each(nz - 1, lambda i: u_z(i).start())

    @pl.when(last)
    def _():
        g_all[x, mine, :] = dx32[...].astype(BF16)
        each(nz - 1, lambda i: g_z(i).start())

    gbx[...] = jnp.zeros_like(gbx)
    ubx[...] = jnp.zeros_like(ubx)
    dax[...] = jnp.zeros_like(dax)
    gbx[0:rank, :] = gb_ref[...]
    ubx[rank : 2 * rank, :] = ub_ref[...]
    dax[:, 0:rank] = da_ref[...]
    wd[hidden + rank : hidden + TILE, :] = jnp.zeros((TILE - rank, width), BF16)

    def placed(tiles, member, block):
        slot = inv[member, block]
        tile = tiles[jnp.maximum(slot, 0)]
        return jnp.where(slot >= 0, tile, jnp.zeros_like(tile))

    loads[0].wait()

    def build_gate(r):
        for c in range(col_blocks):
            wg[aligned(r, TILE), c * TILE : (c + 1) * TILE] = placed(tiles_g, 0, r * col_blocks + c)

    each(row_blocks, build_gate)
    each(nz - 1, lambda i: u_z(i).wait())
    each(nx - 1, lambda i: u_x(i).start())

    @pl.when(last)
    def _():
        each(nz - 1, lambda i: g_z(i).wait())
        each(nx - 1, lambda i: g_x(i).start())

    loads[1].wait()

    def build_up(r):
        for c in range(col_blocks):
            wu[aligned(r, TILE), c * TILE : (c + 1) * TILE] = placed(tiles_u, 1, r * col_blocks + c)

    each(row_blocks, build_up)
    loads[2].wait()

    def build_down(c):
        for r in range(col_blocks):
            wd[r * TILE : (r + 1) * TILE, aligned(c, TILE)] = placed(tiles_d, 2, r * row_blocks + c)

    each(row_blocks, build_down)
    loads[3].wait()
    loads[4].wait()

    each(nx - 1, lambda i: u_x(i).wait())
    acc_g[...] = jnp.zeros_like(acc_g)
    acc_u[...] = jnp.zeros_like(acc_u)

    def forward(k):
        rows = aligned(k, slab)
        acc_g[...] += dot_nn(u_all[k], wg[rows, :])
        acc_u[...] += dot_nn(u_all[k], wu[rows, :])

    each(nx, forward)
    a_gu[...] = acc_g[:, hidden : hidden + TILE].astype(BF16)
    acc_g[:, 0:hidden] += SCALE * dot_nn(a_gu[...], gbx[...])
    acc_u[...] += SCALE * dot_nn(a_gu[...], ubx[...])

    @pl.when(jnp.logical_not(last))
    def _():
        remote(
            dx16, g_all.at[x, mine], y_ss.at[0], y_rs.at[0], pipe=lax.rem(pipe + 1, pipe_n)
        ).wait_recv()
        each(nz - 1, lambda i: g_z(i).start())
        each(nz - 1, lambda i: g_z(i).wait())
        each(nx - 1, lambda i: g_x(i).start())

    each(nx - 1, lambda i: g_x(i).wait())

    acc_d[...] = jnp.zeros_like(acc_d)

    def hidden_grad(k):
        acc_d[...] += dot_nt(g_all[k], wd[:, aligned(k, slab)])

    each(nx, hidden_grad)
    c_lr[...] = acc_d[:, hidden : hidden + TILE].astype(BF16)
    acc_d[:, 0:hidden] += SCALE * dot_nt(c_lr[...], dax[...])

    lane = lax.broadcasted_iota(jnp.int32, (zt, TILE), 1)

    def middle(j):
        rows = aligned(j, zt)
        gate = acc_g[rows, 0:hidden]
        up = acc_u[rows, :]
        dh = acc_d[rows, 0:hidden]
        q = jax.nn.sigmoid(gate)
        active = gate * q
        hid[rows, :] = (active * up).astype(BF16)
        dgate = (dh * up * (q * (1.0 + gate * (1.0 - q)))).astype(BF16)
        dupw = (dh * active).astype(BF16)
        dge[rows, 0:hidden] = dgate
        dup[rows, :] = dupw
        dots = jnp.sum(dgate.astype(F32) * gate + dupw.astype(F32) * up, axis=1, keepdims=True)
        tm[rows, TILE : 2 * TILE] = jnp.where(lane == rank, dots, 0.0)

    each(nz, middle)
    tm[:, 0:TILE] = dot_nt(dge[:, 0:hidden], gbx[...]) + dot_nt(dup[...], ubx[...])
    tm[:, TILE : 2 * TILE] += dot_nn(hid[...], dax[...])
    dge[:, hidden : hidden + TILE] = (SCALE * tm[:, 0:TILE]).astype(BF16)

    def slab_copy(i):
        return remote(
            slab_send.at[i], slab_recv.at[i], rx_ss.at[i], rx_rs.at[i], tensor=x_peer(i + 1)
        )

    def partial(k):
        rows = aligned(k, slab)
        return dot_nt(dge[...], wg[rows, :]) + dot_nt(dup[...], wu[rows, :])

    def send_slab(i):
        slab_send[i, :, 0:slab] = partial(lax.rem(x + i + 1, nx)).astype(BF16)
        slab_send[i, :, slab : slab + EXTRA] = tm[...].astype(BF16)
        slab_copy(i).start()

    each(nx - 1, send_slab)
    total[:, 0:slab] = partial(x)
    total[:, slab : slab + EXTRA] = tm[...]

    ps_send[0:rank, :] = (SCALE * dot_tn(a_gu[...], dge[:, 0:hidden]))[0:rank, :].astype(BF16)
    ps_send[rank : 2 * rank, :] = (SCALE * dot_tn(a_gu[...], dup[...]))[rank : 2 * rank, :].astype(BF16)
    pd_send[...] = (SCALE * dot_tn(hid[...], c_lr[...])).astype(BF16)

    def swap(src, dst, i):
        return remote(src, dst, dp_ss.at[i], dp_rs.at[i], dp=1 - core)

    swap(ps_send, ps_recv, 0).start()
    swap(pd_send, pd_recv, 1).start()

    each(nx - 1, lambda i: slab_copy(i).wait())

    def add_slabs(j):
        rows = aligned(j, zt)
        value = total[rows, :]
        for i in range(nx - 1):
            value = value + slab_recv[i, rows, :].astype(F32)
        total[rows, :] = value
        z_send[rows, :] = value.astype(BF16)

    each(nz, add_slabs)

    def z_copy(i):
        return remote(
            z_send.at[aligned(lax.rem(z + i + 1, nz), zt)],
            z_recv.at[i],
            rz_ss.at[i],
            rz_rs.at[i],
            tensor=z_peer(i + 1),
        )

    each(nz - 1, lambda i: z_copy(i).start())
    each(nz - 1, lambda i: z_copy(i).wait())
    value = total[mine, :]
    for i in range(nz - 1):
        value = value + z_recv[i].astype(F32)

    zm = value[:, slab + TILE : slab + 2 * TILE]
    mean = jnp.sum(jnp.where(lane == rank, zm, 0.0), axis=1, keepdims=True) / width
    dn = value[:, 0:slab] * gain
    row_scale = r16[:, 0:1]
    dx = g_all[x, mine, :].astype(F32) + row_scale * (dn - n16[...] * mean)
    dx16[...] = dx.astype(BF16)

    def y_copy():
        return remote(
            dx16, g_all.at[x, mine], y_ss.at[0], y_rs.at[0], pipe=lax.rem(pipe + pipe_n - 1, pipe_n)
        )

    @pl.when(pipe > 0)
    def _():
        y_copy().start()

    t_all[mine, :] = value[:, slab : slab + EXTRA].astype(BF16)

    def t_z(i):
        return remote(
            t_all.at[mine], t_all.at[mine], tz_ss.at[i], tz_rs.at[i], tensor=z_peer(i + 1)
        )

    each(nz - 1, lambda i: t_z(i).start())

    dx32[...] = dx16[...].astype(F32)
    for k in range(nx):
        o_send[k] = dx32[k * rows_q : (k + 1) * rows_q, :]

    def o_copy(i):
        return remote(
            o_send.at[lax.rem(x + i + 1, nx)],
            o_recv.at[x],
            o_ss.at[i],
            o_rs.at[i],
            tensor=x_peer(i + 1),
        )

    each(nx - 1, lambda i: o_copy(i).start())
    o_recv[x] = o_send[x]

    swap(ps_send, ps_recv, 0).wait()
    swap(pd_send, pd_recv, 1).wait()
    hid_out[...] = (ps_send[...].astype(F32) + ps_recv[...].astype(F32)).astype(BF16)
    da_out[...] = (pd_send[...].astype(F32) + pd_recv[...].astype(F32)).astype(BF16)

    each(nx - 1, lambda i: o_copy(i).wait())
    for k in range(nx):
        dx_out[:, k * slab : (k + 1) * slab] = o_recv[k].astype(BF16)

    each(nz - 1, lambda i: t_z(i).wait())

    def wide(k):
        pa_send[aligned(k, slab), :] = (SCALE * dot_tn(u_all[k], t_all[:, 0:TILE])).astype(BF16)
        pb_send[:, aligned(k, slab)] = (
            SCALE * dot_tn(t_all[:, TILE : 2 * TILE], g_all[k])
        )[0:rank, :].astype(BF16)

    each(nx, wide)
    swap(pa_send, pa_recv, 2).start()
    swap(pb_send, pb_recv, 3).start()
    swap(pa_send, pa_recv, 2).wait()
    swap(pb_send, pb_recv, 3).wait()

    def wide_out(k):
        rows = aligned(k, slab)
        ab_out[rows, :] = (pa_send[rows, :].astype(F32) + pa_recv[rows, :].astype(F32)).astype(BF16)
        db_out[:, rows] = (pb_send[:, rows].astype(F32) + pb_recv[:, rows].astype(F32)).astype(BF16)

    each(nx, wide_out)

    @pl.when(pipe > 0)
    def _():
        y_copy().wait_send()


def shards(
    states,
    out_grad,
    norm_gain,
    gate_tiles,
    up_tiles,
    down_tiles,
    tile_lists,
    tile_counts,
    gate_a,
    gate_adapter_output,
    up_a,
    upper_adapter_output,
    down_adapter_input,
    down_b,
):
    pipe_n = lax.axis_size("pipe")
    tensor_n = lax.axis_size("tensor")
    nx = X_CHIPS
    nz = tensor_n // nx
    rows_q, width = states.shape[2:]
    slots = gate_tiles.shape[1]
    rank = gate_a.shape[2]
    hidden = gate_adapter_output.shape[2]
    tokens = rows_q * tensor_n
    zt = rows_q * nx
    slab = width // nx
    row_blocks, col_blocks = width // TILE, hidden // TILE
    blocks = row_blocks * col_blocks

    places = tile_lists[0]
    strides = jnp.array([col_blocks, col_blocks, row_blocks], jnp.int32)[:, None]
    place = places[:, :, 0] * strides + places[:, :, 1]
    slot_ids = jnp.arange(slots, dtype=jnp.int32)
    alive = slot_ids[None, :] < tile_counts[0]
    hit = jnp.logical_and(
        place[:, None, :] == jnp.arange(blocks, dtype=jnp.int32)[None, :, None], alive[:, None, :]
    )
    inv = jnp.max(jnp.where(hit, slot_ids[None, None, :], -1), axis=2)
    ab = jnp.concatenate([gate_a[0], up_a[0]], axis=1)

    vmem = pl.BlockSpec(memory_space=pltpu.VMEM)
    anywhere = pl.BlockSpec(memory_space=pl.ANY)
    smem = pl.BlockSpec(memory_space=pltpu.SMEM)
    dma = pltpu.SemaphoreType.DMA
    ext = hidden + TILE
    scratch = [
        pltpu.VMEM((slots, TILE, TILE), BF16),
        pltpu.VMEM((slots, TILE, TILE), BF16),
        pltpu.VMEM((slots, TILE, TILE), BF16),
        pltpu.VMEM((width, ext), BF16),
        pltpu.VMEM((width, hidden), BF16),
        pltpu.VMEM((ext, width), BF16),
        pltpu.VMEM((TILE, hidden), BF16),
        pltpu.VMEM((TILE, hidden), BF16),
        pltpu.VMEM((hidden, TILE), BF16),
        pltpu.VMEM((nx, rows_q, 2 * slab + TILE), F32),
        pltpu.VMEM((nx, rows_q, 2 * slab + TILE), F32),
        pltpu.VMEM((zt, slab), F32),
        pltpu.VMEM((zt, TILE), F32),
        pltpu.VMEM((nx, tokens, slab), BF16),
        pltpu.VMEM((nx, tokens, slab), BF16),
        pltpu.VMEM((tokens, ext), F32),
        pltpu.VMEM((tokens, hidden), F32),
        pltpu.VMEM((tokens, ext), F32),
        pltpu.VMEM((tokens, TILE), BF16),
        pltpu.VMEM((tokens, TILE), BF16),
        pltpu.VMEM((tokens, hidden), BF16),
        pltpu.VMEM((tokens, ext), BF16),
        pltpu.VMEM((tokens, hidden), BF16),
        pltpu.VMEM((tokens, EXTRA), F32),
        pltpu.VMEM((nx - 1, tokens, slab + EXTRA), BF16),
        pltpu.VMEM((nx - 1, tokens, slab + EXTRA), BF16),
        pltpu.VMEM((tokens, slab + EXTRA), F32),
        pltpu.VMEM((tokens, slab + EXTRA), BF16),
        pltpu.VMEM((nz - 1, zt, slab + EXTRA), BF16),
        pltpu.VMEM((zt, slab), BF16),
        pltpu.VMEM((zt, slab), F32),
        pltpu.VMEM((nx, rows_q, slab), F32),
        pltpu.VMEM((nx, rows_q, slab), F32),
        pltpu.VMEM((tokens, EXTRA), BF16),
        pltpu.VMEM((width, TILE), BF16),
        pltpu.VMEM((width, TILE), BF16),
        pltpu.VMEM((rank, width), BF16),
        pltpu.VMEM((rank, width), BF16),
        pltpu.VMEM((2 * rank, hidden), BF16),
        pltpu.VMEM((2 * rank, hidden), BF16),
        pltpu.VMEM((hidden, TILE), BF16),
        pltpu.VMEM((hidden, TILE), BF16),
        dma((5,)),
    ]
    for count in (nx - 1, nz - 1, nx - 1, nz - 1, nx - 1, 1, nx - 1, nz - 1, nx - 1, nz - 1, 4):
        scratch += [dma((count,)), dma((count,))]
    dx, ab_grad, hid_grad, da_grad, db_grad = pl.pallas_call(
        functools.partial(section_kernel, (pipe_n, nz, nx, hidden, width)),
        out_shape=(
            jax.ShapeDtypeStruct((rows_q, width), BF16),
            jax.ShapeDtypeStruct((width, 2 * rank), BF16),
            jax.ShapeDtypeStruct((2 * rank, hidden), BF16),
            jax.ShapeDtypeStruct((hidden, TILE), BF16),
            jax.ShapeDtypeStruct((rank, width), BF16),
        ),
        in_specs=[smem, vmem, vmem, vmem] + [anywhere] * 4 + [vmem] * 3 + [anywhere],
        out_specs=[vmem] * 5,
        scratch_shapes=scratch,
        compiler_params=pltpu.CompilerParams(
            collective_id=0, has_side_effects=True, vmem_limit_bytes=56 * 1024 * 1024
        ),
        cost_estimate=pl.CostEstimate(
            flops=10 * tokens * width * hidden,
            bytes_accessed=6 * slots * TILE * TILE,
            transcendentals=tokens * hidden,
        ),
    )(
        inv,
        states[0, 0],
        out_grad[0],
        norm_gain,
        gate_tiles[0],
        up_tiles[0],
        down_tiles[0],
        ab,
        gate_adapter_output[0],
        upper_adapter_output[0],
        down_adapter_input[0],
        down_b[0],
    )
    return (
        dx[None, None],
        ab_grad[None, :, :rank],
        hid_grad[None, :rank],
        ab_grad[None, :, rank:],
        hid_grad[None, rank:],
        da_grad[None, :, :rank],
        db_grad[None],
    )


def solution(mesh):
    placed = (
        P("pipe", "dp", "tensor", None),
        P("dp", "tensor", None),
        P("pipe", None),
        P("pipe", "tensor", None, None),
        P("pipe", "tensor", None, None),
        P("pipe", "tensor", None, None),
        P("pipe", None, "tensor", None),
        P("pipe", None, "tensor"),
        P("pipe", None, None),
        P("pipe", None, "tensor"),
        P("pipe", None, None),
        P("pipe", None, "tensor"),
        P("pipe", "tensor", None),
        P("pipe", None, None),
    )
    return jax.shard_map(
        shards,
        mesh=mesh,
        in_specs=placed,
        out_specs=(
            P("pipe", "dp", "tensor", None),
            P("pipe", None, None),
            P("pipe", None, "tensor"),
            P("pipe", None, None),
            P("pipe", None, "tensor"),
            P("pipe", "tensor", None),
            P("pipe", None, None),
        ),
        check_vma=False,
    )
```

```python
import functools

import jax
import jax.numpy as jnp
from jax import lax
from jax.experimental import pallas as pl
from jax.experimental.pallas import tpu as pltpu
from jax.sharding import PartitionSpec as P

MESH = pl.DeviceIdType.MESH
F32 = jnp.float32
BF16 = jnp.bfloat16
EPSILON = 1e-05
SCALE = 0.25
X_CHIPS = 4
TILE = 128
EXTRA = 256


def dot_nn(a, b):
    return lax.dot_general(a, b, (((1,), (0,)), ((), ())), preferred_element_type=F32)


def dot_nt(a, b):
    return lax.dot_general(a, b, (((1,), (1,)), ((), ())), preferred_element_type=F32)


def dot_tn(a, b):
    return lax.dot_general(a, b, (((0,), (0,)), ((), ())), preferred_element_type=F32)


def each(count, body):
    def step(i, carry):
        body(i)
        return carry

    lax.fori_loop(0, count, step, 0)


def aligned(index, size):
    return pl.ds(pl.multiple_of(index * size, size), size)


def section_kernel(
    sizes,
    inv,
    x_ref,
    go_ref,
    gain_ref,
    gate_hbm,
    up_hbm,
    down_hbm,
    ga_hbm,
    ua_hbm,
    db_hbm,
    gb_ref,
    ub_ref,
    da_ref,
    dx_out,
    wide_own,
    wide_recv,
    hid_own,
    hid_recv,
    tiles_g,
    tiles_u,
    tiles_d,
    wgu,
    wd,
    ab,
    gub,
    dax,
    a2a_send,
    a2a_recv,
    n16,
    r16,
    dx32,
    dx16,
    u_all,
    g_all,
    acc_gu,
    acc_a,
    acc_d,
    a_gu,
    c_lr,
    hid,
    dgu,
    ta,
    tm,
    m_send,
    m_recv,
    s_far,
    r_far,
    s_near,
    r_near,
    total,
    z_send,
    z_recv,
    o_send,
    o_recv,
    t_send,
    t_recv,
    tz_send,
    tz_recv,
    t_all,
    load_sem,
    a2a_ss,
    a2a_rs,
    uz_ss,
    uz_rs,
    ud_ss,
    ud_rs,
    ur_ss,
    ur_rs,
    gz_ss,
    gz_rs,
    gd_ss,
    gd_rs,
    gr_ss,
    gr_rs,
    m_ss,
    m_rs,
    far_ss,
    far_rs,
    near_ss,
    near_rs,
    rz_ss,
    rz_rs,
    o_ss,
    o_rs,
    tx_ss,
    tx_rs,
    tr_ss,
    tr_rs,
    ta_ss,
    ta_rs,
    dp_ss,
    dp_rs,
):
    pipe_n, nz, nx, hidden, width = sizes
    slab = width // nx
    half = slab // 2
    quarter = slab // 4
    rows_q = x_ref.shape[0]
    zt = rows_q * nx
    col_blocks = hidden // TILE
    row_blocks = width // TILE
    rank = gb_ref.shape[0]
    pipe = lax.axis_index("pipe")
    tensor = lax.axis_index("tensor")
    core = lax.axis_index("dp")
    z = tensor // nx
    x = lax.rem(tensor, nx)
    last = pipe == pipe_n - 1
    below = lax.rem(pipe + pipe_n - 1, pipe_n)
    above = lax.rem(pipe + 1, pipe_n)
    right = lax.rem(x + 1, nx)
    left = lax.rem(x + nx - 1, nx)
    across = lax.rem(x + 2, nx)

    def remote(src, dst, ss, rs, **where):
        return pltpu.make_async_remote_copy(
            src_ref=src, dst_ref=dst, send_sem=ss, recv_sem=rs, device_id=where, device_id_type=MESH
        )

    def x_peer(i):
        return z * nx + lax.rem(x + i, nx)

    def z_peer(i):
        return lax.rem(z + i, nz) * nx + x

    def side_peer(side):
        return z * nx + (right if side == 0 else left)

    barrier = pltpu.get_barrier_semaphore()

    def greet(**where):
        pl.semaphore_signal(barrier, inc=1, device_id=where, device_id_type=MESH)

    each(nx - 1, lambda i: greet(tensor=x_peer(i + 1)))
    each(nz - 1, lambda i: greet(tensor=z_peer(i + 1)))
    greet(dp=1 - core)
    each(nz, lambda i: greet(pipe=above, tensor=z_peer(i)))
    each(nz, lambda i: greet(pipe=below, tensor=z_peer(i)))

    loads = [
        pltpu.make_async_copy(gate_hbm, tiles_g, load_sem.at[0]),
        pltpu.make_async_copy(up_hbm, tiles_u, load_sem.at[1]),
        pltpu.make_async_copy(down_hbm, tiles_d, load_sem.at[2]),
        pltpu.make_async_copy(ga_hbm, ab.at[pl.ds(0, rank), :], load_sem.at[3]),
        pltpu.make_async_copy(ua_hbm, ab.at[pl.ds(rank, rank), :], load_sem.at[4]),
        pltpu.make_async_copy(db_hbm, wd.at[pl.ds(hidden, rank), :], load_sem.at[5]),
    ]
    for load in loads:
        load.start()

    xin = x_ref[...].astype(F32)
    scale_rms = lax.rsqrt(jnp.mean(xin * xin, axis=1, keepdims=True) + EPSILON)
    normed = xin * scale_rms
    given = go_ref[...].astype(F32)
    for k in range(nx):
        a2a_send[k, :, 0:slab] = normed[:, k * slab : (k + 1) * slab]
        a2a_send[k, :, slab : 2 * slab] = given[:, k * slab : (k + 1) * slab]
        a2a_send[k, :, 2 * slab : 2 * slab + TILE] = jnp.broadcast_to(scale_rms, (rows_q, TILE))

    pl.semaphore_wait(barrier, (nx - 1) + (nz - 1) + 1 + 2 * nz)

    def a2a(i):
        return remote(
            a2a_send.at[lax.rem(x + i + 1, nx)],
            a2a_recv.at[x],
            a2a_ss.at[i],
            a2a_rs.at[i],
            tensor=x_peer(i + 1),
        )

    each(nx - 1, lambda i: a2a(i).start())
    a2a_recv[x] = a2a_send[x]
    each(nx - 1, lambda i: a2a(i).wait())
    for k in range(nx):
        n16[k * rows_q : (k + 1) * rows_q, :] = a2a_recv[k, :, 0:slab]
        dx32[k * rows_q : (k + 1) * rows_q, :] = a2a_recv[k, :, slab : 2 * slab]
        r16[k * rows_q : (k + 1) * rows_q, :] = a2a_recv[k, :, 2 * slab : 2 * slab + TILE]
    gain = gain_ref[:, aligned(x, slab)].astype(F32)
    mine = aligned(z, zt)
    u_all[x, mine, :] = (n16[...] * gain).astype(BF16)

    def cols(h):
        return pl.ds(h * half, half)

    def u_z(h, i):
        place = u_all.at[x, mine, cols(h)]
        return remote(
            place, place, uz_ss.at[h * nz + i], uz_rs.at[h * nz + z], tensor=z_peer(i + 1)
        )

    def given_z(h, i):
        place = g_all.at[x, mine, cols(h)]
        return remote(
            place, place, gz_ss.at[h * nz + i], gz_rs.at[h * nz + z], tensor=z_peer(i + 1)
        )

    def sent_z(h, i):
        return remote(
            dx16.at[:, cols(h)],
            g_all.at[x, mine, cols(h)],
            gz_ss.at[h * nz + i],
            gz_rs.at[h * nz + z],
            pipe=below,
            tensor=z_peer(i),
        )

    def came_z(buf, rs, h, source):
        place = buf.at[x, aligned(source, zt), cols(h)]
        remote(place, place, rs.at[h * nz + source], rs.at[h * nz + source], pipe=above).wait_recv()

    def direct(buf, ss, rs, side, h):
        place = buf.at[x, :, cols(h)]
        return remote(
            place, place, ss.at[side * 2 + h], rs.at[side * 2 + h], tensor=side_peer(side)
        )

    def relay(buf, ss, rs, side, h):
        place = buf.at[left if side == 0 else right, :, pl.ds((2 * h + side) * quarter, quarter)]
        return remote(
            place, place, ss.at[side * 2 + h], rs.at[side * 2 + h], tensor=side_peer(side)
        )

    def send_direct(buf, ss, rs, wait_z):
        for h in range(2):
            wait_z(h)
            for side in range(2):
                direct(buf, ss, rs, side, h).start()

    def send_relays(buf, dss, drs, rss, rrs):
        for h in range(2):
            for side in range(2):
                direct(buf, dss, drs, side, h).wait_recv()
                relay(buf, rss, rrs, side, h).start()

    for h in range(2):
        each(nz - 1, lambda i: u_z(h, i).start())

    @pl.when(last)
    def _():
        g_all[x, mine, :] = dx32[...].astype(BF16)
        for h in range(2):
            each(nz - 1, lambda i: given_z(h, i).start())

    gub[...] = jnp.zeros_like(gub)
    dax[...] = jnp.zeros_like(dax)
    gub[0:rank, 0:hidden] = gb_ref[...]
    gub[rank : 2 * rank, hidden : 2 * hidden] = ub_ref[...]
    dax[0:rank, :] = da_ref[...]
    wd[hidden + rank : hidden + TILE, :] = jnp.zeros((TILE - rank, width), BF16)

    def placed(tiles, member, block):
        slot = inv[member, block]
        tile = tiles[jnp.maximum(slot, 0)]
        return jnp.where(slot >= 0, tile, jnp.zeros_like(tile))

    loads[0].wait()

    def build_gate(r):
        for c in range(col_blocks):
            wgu[aligned(r, TILE), c * TILE : (c + 1) * TILE] = placed(tiles_g, 0, r * col_blocks + c)

    each(row_blocks, build_gate)

    def own_u_z(h):
        each(nz - 1, lambda i: came_z(u_all, uz_rs, h, lax.rem(z + i + 1, nz)))

    send_direct(u_all, ud_ss, ud_rs, own_u_z)

    loads[1].wait()

    def build_up(r):
        for c in range(col_blocks):
            wgu[aligned(r, TILE), hidden + c * TILE : hidden + (c + 1) * TILE] = placed(
                tiles_u, 1, r * col_blocks + c
            )

    each(row_blocks, build_up)
    send_relays(u_all, ud_ss, ud_rs, ur_ss, ur_rs)
    loads[2].wait()

    def build_down(c):
        for r in range(col_blocks):
            wd[r * TILE : (r + 1) * TILE, aligned(c, TILE)] = placed(tiles_d, 2, r * row_blocks + c)

    each(row_blocks, build_down)
    for load in loads[3:]:
        load.wait()

    def given_came(h):
        each(nz - 1, lambda i: came_z(g_all, gz_rs, h, lax.rem(z + i + 1, nz)))

    def sent_came(h):
        each(nz, lambda i: came_z(g_all, gz_rs, h, i))

    @pl.when(last)
    def _():
        send_direct(g_all, gd_ss, gd_rs, given_came)

    acc_gu[...] = jnp.zeros_like(acc_gu)
    acc_a[...] = jnp.zeros_like(acc_a)

    def forward(i):
        k = lax.rem(x + jnp.where(i == 2, 3, jnp.where(i == 3, 2, i)), nx)

        @pl.when(i == 3)
        def _():
            for h in range(2):
                for side in range(2):
                    relay(u_all, ur_ss, ur_rs, side, h).wait_recv()

        acc_gu[...] += dot_nn(u_all[k], wgu[aligned(k, slab), :])
        acc_a[...] += dot_nt(u_all[k], ab[:, aligned(k, slab)])

    each(nx, forward)
    a_gu[...] = acc_a[...].astype(BF16)
    acc_gu[...] += SCALE * dot_nn(a_gu[...], gub[...])

    @pl.when(jnp.logical_not(last))
    def _():
        send_direct(g_all, gd_ss, gd_rs, sent_came)

    acc_d[...] = jnp.zeros_like(acc_d)

    def hidden_grad(i):
        k = lax.rem(x + jnp.where(i == 2, 3, jnp.where(i == 3, 2, i)), nx)

        @pl.when(i == 1)
        def _():
            send_relays(g_all, gd_ss, gd_rs, gr_ss, gr_rs)

        @pl.when(i == 3)
        def _():
            for h in range(2):
                for side in range(2):
                    relay(g_all, gr_ss, gr_rs, side, h).wait_recv()

        acc_d[...] += dot_nt(g_all[k], wd[:, aligned(k, slab)])

    each(nx, hidden_grad)
    c_lr[...] = acc_d[:, hidden : hidden + TILE].astype(BF16)
    acc_d[:, 0:hidden] += SCALE * dot_nn(c_lr[...], dax[...])

    lane = lax.broadcasted_iota(jnp.int32, (zt, TILE), 1)
    row = lax.broadcasted_iota(jnp.int32, (zt, TILE), 0)
    m_send[...] = jnp.zeros_like(m_send)

    def middle(j):
        rows = aligned(j, zt)
        gate = acc_gu[rows, 0:hidden]
        up = acc_gu[rows, hidden : 2 * hidden]
        dh = acc_d[rows, 0:hidden]
        q = jax.nn.sigmoid(gate)
        active = gate * q
        hid[rows, :] = (active * up).astype(BF16)
        dgate = (dh * up * (q * (1.0 + gate * (1.0 - q)))).astype(BF16)
        dup = (dh * active).astype(BF16)
        dgu[rows, 0:hidden] = dgate
        dgu[rows, hidden : 2 * hidden] = dup
        dots = jnp.sum(dgate.astype(F32) * gate + dup.astype(F32) * up, axis=1, keepdims=True)
        spread = jnp.sum(jnp.where(lane == row + j * zt, dots, 0.0), axis=0, keepdims=True)
        m_send[...] += jnp.broadcast_to(spread, m_send.shape)

    each(nz, middle)

    def m_copy(i):
        return remote(m_send, m_recv.at[i], m_ss.at[i], m_rs.at[i], tensor=x_peer(i + 1))

    each(nx - 1, lambda i: m_copy(i).start())
    tm[:, 0:TILE] = dot_nt(dgu[...], gub[...])
    ta[...] = (SCALE * tm[:, 0:TILE]).astype(BF16)

    def partial(k):
        return dot_nt(dgu[...], wgu[aligned(k, slab), :]) + dot_nn(ta[...], ab[:, aligned(k, slab)])

    def part(q):
        return pl.ds(q * quarter, quarter)

    def far(side, h):
        return remote(
            s_far.at[:, part(2 * h + side)],
            r_far.at[side, h],
            far_ss.at[side * 2 + h],
            far_rs.at[side * 2 + h],
            tensor=side_peer(side),
        )

    def near(side, q):
        return remote(
            s_near.at[side, :, part(q)],
            r_near.at[side, :, part(q)],
            near_ss.at[side * 4 + q],
            near_rs.at[side * 4 + q],
            tensor=side_peer(side),
        )

    s_far[...] = partial(across).astype(BF16)
    for h in range(2):
        for side in range(2):
            far(side, h).start()

    s_near[0] = partial(right).astype(BF16)
    near(0, 1).start()
    s_near[1] = partial(left).astype(BF16)
    near(1, 0).start()
    total[...] = partial(x)

    for h in range(2):
        for side in range(2):
            q = 2 * h + side
            far(side, h).wait_recv()
            s_near[side, :, part(q)] = (
                s_near[side, :, part(q)].astype(F32) + r_far[side, h].astype(F32)
            ).astype(BF16)
            near(side, q).start()
        if h == 0:
            near(0, 3).start()
            near(1, 2).start()

    tm[:, TILE : 2 * TILE] = dot_nt(hid[...], dax[...])
    t_send[...] = tm[...].astype(BF16)
    grads = SCALE * dot_tn(a_gu[...], dgu[...])
    hid_own[0:rank, :] = grads[0:rank, 0:hidden].astype(BF16)
    hid_own[rank : 2 * rank, :] = grads[rank : 2 * rank, hidden : 2 * hidden].astype(BF16)
    hid_own[2 * rank : 3 * rank, :] = (SCALE * dot_tn(c_lr[...], hid[...]))[0:rank, :].astype(BF16)

    def swap(src, dst, i):
        return remote(src, dst, dp_ss.at[i], dp_rs.at[i], dp=1 - core)

    swap(hid_own, hid_recv, 0).start()

    def z_lanes(h):
        return pl.ds(0, TILE + half) if h == 0 else pl.ds(TILE + half, half)

    def z_copy(h, i):
        return remote(
            z_send.at[aligned(lax.rem(z + i + 1, nz), zt), z_lanes(h)],
            z_recv.at[i, :, z_lanes(h)],
            rz_ss.at[h * nz + i],
            rz_rs.at[h * nz + i],
            tensor=z_peer(i + 1),
        )

    each(nx - 1, lambda i: m_copy(i).wait())
    dots_row = m_send[...]
    for i in range(nx - 1):
        dots_row = dots_row + m_recv[i]
    m_send[...] = dots_row

    for h in range(2):
        for q in (2 * h, 2 * h + 1):
            for side in range(2):
                near(side, q).wait_recv()

        def add_slabs(j):
            rows = aligned(j, zt)
            value = (
                total[rows, cols(h)]
                + r_near[0, rows, cols(h)].astype(F32)
                + r_near[1, rows, cols(h)].astype(F32)
            )
            total[rows, cols(h)] = value
            z_send[rows, pl.ds(TILE + h * half, half)] = value.astype(BF16)
            if h == 0:
                column = jnp.sum(
                    jnp.where(lane == row + j * zt, m_send[0:1, :], 0.0), axis=1, keepdims=True
                )
                z_send[rows, 0:TILE] = jnp.broadcast_to(column, (zt, TILE)).astype(BF16)

        each(nz, add_slabs)
        each(nz - 1, lambda i: z_copy(h, i).start())

    def t_x(i):
        return remote(t_send, t_recv.at[i], tx_ss.at[i], tx_rs.at[i], tensor=x_peer(i + 1))

    each(nx - 1, lambda i: t_x(i).start())

    row_scale = r16[:, 0:1]
    mean = None
    for h in range(2):
        each(nz - 1, lambda i: z_copy(h, i).wait_recv())
        if h == 0:
            mean = z_send[mine, 0:TILE].astype(F32)
            for i in range(nz - 1):
                mean = mean + z_recv[i, :, 0:TILE].astype(F32)
            mean = mean[:, 0:1] / width
        value = total[mine, cols(h)]
        for i in range(nz - 1):
            value = value + z_recv[i, :, pl.ds(TILE + h * half, half)].astype(F32)
        dn = value * gain[:, h * half : (h + 1) * half]
        dx = g_all[x, mine, cols(h)].astype(F32) + row_scale * (dn - n16[:, cols(h)] * mean)
        dx16[:, cols(h)] = dx.astype(BF16)

        @pl.when(pipe > 0)
        def _():
            each(nz, lambda i: sent_z(h, i).start())

    each(nx - 1, lambda i: t_x(i).wait())
    t_sum = tm[...]
    for i in range(nx - 1):
        t_sum = t_sum + t_recv[i].astype(F32)
    tm[...] = t_sum
    tz_send[...] = t_sum.astype(BF16)

    def t_reduce(i):
        return remote(
            tz_send.at[aligned(lax.rem(z + i + 1, nz), zt)],
            tz_recv.at[i],
            tr_ss.at[i],
            tr_rs.at[i],
            tensor=z_peer(i + 1),
        )

    each(nz - 1, lambda i: t_reduce(i).start())

    dx32[...] = dx16[...].astype(F32)
    for k in range(nx):
        o_send[k] = dx32[k * rows_q : (k + 1) * rows_q, :]

    def o_copy(i):
        return remote(
            o_send.at[lax.rem(x + i + 1, nx)],
            o_recv.at[x],
            o_ss.at[i],
            o_rs.at[i],
            tensor=x_peer(i + 1),
        )

    each(nx - 1, lambda i: o_copy(i).start())
    o_recv[x] = o_send[x]

    each(nz - 1, lambda i: t_reduce(i).wait())
    t_mine = tm[mine, :]
    for i in range(nz - 1):
        t_mine = t_mine + tz_recv[i].astype(F32)
    t_all[mine, :] = t_mine.astype(BF16)

    def t_gather(i):
        return remote(
            t_all.at[mine], t_all.at[mine], ta_ss.at[i], ta_rs.at[i], tensor=z_peer(i + 1)
        )

    each(nz - 1, lambda i: t_gather(i).start())

    each(nx - 1, lambda i: o_copy(i).wait())
    for k in range(nx):
        dx_out[:, k * slab : (k + 1) * slab] = o_recv[k].astype(BF16)

    each(nz - 1, lambda i: t_gather(i).wait())

    def wide(k):
        columns = aligned(k, slab)
        wide_own[0 : 2 * rank, columns] = (
            SCALE * dot_tn(t_all[:, 0:TILE], u_all[k])
        ).astype(BF16)
        wide_own[2 * rank : 3 * rank, columns] = (
            SCALE * dot_tn(t_all[:, TILE : 2 * TILE], g_all[k])
        )[0:rank, :].astype(BF16)

    each(nx, wide)
    swap(wide_own, wide_recv, 1).start()

    for h in range(2):
        each(nz - 1, lambda i: u_z(h, i).wait_send())
        each(nz - 1, lambda i: z_copy(h, i).wait_send())
        for side in range(2):
            direct(u_all, ud_ss, ud_rs, side, h).wait_send()
            relay(u_all, ur_ss, ur_rs, side, h).wait_send()
            direct(g_all, gd_ss, gd_rs, side, h).wait_send()
            relay(g_all, gr_ss, gr_rs, side, h).wait_send()
            far(side, h).wait_send()
    for q in range(4):
        for side in range(2):
            near(side, q).wait_send()

    @pl.when(last)
    def _():
        for h in range(2):
            each(nz - 1, lambda i: given_z(h, i).wait_send())

    @pl.when(pipe > 0)
    def _():
        for h in range(2):
            each(nz, lambda i: sent_z(h, i).wait_send())

    swap(hid_own, hid_recv, 0).wait()
    swap(wide_own, wide_recv, 1).wait()


def finish_kernel(
    dx, wide_own, wide_recv, hid_own, hid_recv, dx_out, ga_out, ua_out, db_out, gb_out, ub_out, da_out
):
    rank = ga_out.shape[0]
    dx_out[...] = dx[...]
    for index, out in enumerate((ga_out, ua_out, db_out)):
        rows = slice(index * rank, (index + 1) * rank)
        out[...] = (wide_own[rows, :].astype(F32) + wide_recv[rows, :].astype(F32)).astype(BF16)
    for index, out in enumerate((gb_out, ub_out, da_out)):
        rows = slice(index * rank, (index + 1) * rank)
        out[...] = (hid_own[rows, :].astype(F32) + hid_recv[rows, :].astype(F32)).astype(BF16)


def shards(
    states,
    out_grad,
    norm_gain,
    gate_tiles,
    up_tiles,
    down_tiles,
    tile_lists,
    tile_counts,
    gate_a,
    gate_adapter_output,
    up_a,
    upper_adapter_output,
    down_adapter_input,
    down_b,
):
    pipe_n = lax.axis_size("pipe")
    tensor_n = lax.axis_size("tensor")
    nx = X_CHIPS
    nz = tensor_n // nx
    rows_q, width = states.shape[2:]
    slots = gate_tiles.shape[1]
    rank = gate_a.shape[2]
    hidden = gate_adapter_output.shape[2]
    tokens = rows_q * tensor_n
    zt = rows_q * nx
    slab = width // nx
    row_blocks, col_blocks = width // TILE, hidden // TILE
    blocks = row_blocks * col_blocks

    places = tile_lists[0]
    strides = jnp.array([col_blocks, col_blocks, row_blocks], jnp.int32)[:, None]
    place = places[:, :, 0] * strides + places[:, :, 1]
    slot_ids = jnp.arange(slots, dtype=jnp.int32)
    alive = slot_ids[None, :] < tile_counts[0]
    hit = jnp.logical_and(
        place[:, None, :] == jnp.arange(blocks, dtype=jnp.int32)[None, :, None], alive[:, None, :]
    )
    inv = jnp.max(jnp.where(hit, slot_ids[None, None, :], -1), axis=2)

    vmem = pl.BlockSpec(memory_space=pltpu.VMEM)
    anywhere = pl.BlockSpec(memory_space=pl.ANY)
    smem = pl.BlockSpec(memory_space=pltpu.SMEM)
    dma = pltpu.SemaphoreType.DMA
    vm = pltpu.VMEM
    scratch = [
        vm((slots, TILE, TILE), BF16),
        vm((slots, TILE, TILE), BF16),
        vm((slots, TILE, TILE), BF16),
        vm((width, 2 * hidden), BF16),
        vm((hidden + TILE, width), BF16),
        vm((TILE, width), BF16),
        vm((TILE, 2 * hidden), BF16),
        vm((TILE, hidden), BF16),
        vm((nx, rows_q, 2 * slab + TILE), F32),
        vm((nx, rows_q, 2 * slab + TILE), F32),
        vm((zt, slab), F32),
        vm((zt, TILE), F32),
        vm((zt, slab), F32),
        vm((zt, slab), BF16),
        vm((nx, tokens, slab), BF16),
        vm((nx, tokens, slab), BF16),
        vm((tokens, 2 * hidden), F32),
        vm((tokens, TILE), F32),
        vm((tokens, hidden + TILE), F32),
        vm((tokens, TILE), BF16),
        vm((tokens, TILE), BF16),
        vm((tokens, hidden), BF16),
        vm((tokens, 2 * hidden), BF16),
        vm((tokens, TILE), BF16),
        vm((tokens, EXTRA), F32),
        vm((8, TILE), F32),
        vm((nx - 1, 8, TILE), F32),
        vm((tokens, slab), BF16),
        vm((2, 2, tokens, slab // 4), BF16),
        vm((2, tokens, slab), BF16),
        vm((2, tokens, slab), BF16),
        vm((tokens, slab), F32),
        vm((tokens, TILE + slab), BF16),
        vm((nz - 1, zt, TILE + slab), BF16),
        vm((nx, rows_q, slab), F32),
        vm((nx, rows_q, slab), F32),
        vm((tokens, EXTRA), BF16),
        vm((nx - 1, tokens, EXTRA), BF16),
        vm((tokens, EXTRA), BF16),
        vm((nz - 1, zt, EXTRA), BF16),
        vm((tokens, EXTRA), BF16),
        dma((6,)),
    ]
    x_n, z_n, z_2 = nx - 1, nz - 1, 2 * nz
    for count in (x_n, z_2, 4, 4, z_2, 4, 4, x_n, 4, 8, z_2, x_n, x_n, z_n, z_n, 2):
        scratch += [dma((count,)), dma((count,))]
    dx, wide_own, wide_recv, hid_own, hid_recv = pl.pallas_call(
        functools.partial(section_kernel, (pipe_n, nz, nx, hidden, width)),
        out_shape=(
            jax.ShapeDtypeStruct((rows_q, width), BF16),
            jax.ShapeDtypeStruct((3 * rank, width), BF16),
            jax.ShapeDtypeStruct((3 * rank, width), BF16),
            jax.ShapeDtypeStruct((3 * rank, hidden), BF16),
            jax.ShapeDtypeStruct((3 * rank, hidden), BF16),
        ),
        in_specs=[smem, vmem, vmem, vmem] + [anywhere] * 6 + [vmem] * 3,
        out_specs=[vmem] * 5,
        scratch_shapes=scratch,
        compiler_params=pltpu.CompilerParams(
            collective_id=0, has_side_effects=True, vmem_limit_bytes=56 * 1024 * 1024
        ),
        cost_estimate=pl.CostEstimate(
            flops=10 * tokens * width * hidden,
            bytes_accessed=6 * slots * TILE * TILE,
            transcendentals=tokens * hidden,
        ),
    )(
        inv,
        states[0, 0],
        out_grad[0],
        norm_gain,
        gate_tiles[0],
        up_tiles[0],
        down_tiles[0],
        gate_a[0].T,
        up_a[0].T,
        down_b[0],
        gate_adapter_output[0],
        upper_adapter_output[0],
        down_adapter_input[0].T,
    )
    full = jax.ShapeDtypeStruct((rank, width), BF16)
    part = jax.ShapeDtypeStruct((rank, hidden), BF16)
    dx, ga, ua, db, gb, ub, da = pl.pallas_call(
        finish_kernel,
        out_shape=(jax.ShapeDtypeStruct((rows_q, width), BF16), full, full, full, part, part, part),
        in_specs=[vmem] * 5,
        out_specs=[vmem] * 7,
    )(dx, wide_own, wide_recv, hid_own, hid_recv)
    return dx[None, None], ga.T[None], gb[None], ua.T[None], ub[None], da.T[None], db[None]


def solution(mesh):
    placed = (
        P("pipe", "dp", "tensor", None),
        P("dp", "tensor", None),
        P("pipe", None),
        P("pipe", "tensor", None, None),
        P("pipe", "tensor", None, None),
        P("pipe", "tensor", None, None),
        P("pipe", None, "tensor", None),
        P("pipe", None, "tensor"),
        P("pipe", None, None),
        P("pipe", None, "tensor"),
        P("pipe", None, None),
        P("pipe", None, "tensor"),
        P("pipe", "tensor", None),
        P("pipe", None, None),
    )
    return jax.shard_map(
        shards,
        mesh=mesh,
        in_specs=placed,
        out_specs=(
            P("pipe", "dp", "tensor", None),
            P("pipe", None, None),
            P("pipe", None, "tensor"),
            P("pipe", None, None),
            P("pipe", None, "tensor"),
            P("pipe", "tensor", None),
            P("pipe", None, None),
        ),
        check_vma=False,
    )
```
